32 devices in a mesh: member: 2 (over core), tile: 16 (over z, y, x).
Axes of the slice: x: 2, y: 2, z: 4, core: 2. Of those that a mesh axis runs over, the one named last changes fastest.
Arguments:
- winds: bfloat16 [8, 4, 2, 256, 2048], P('member', None, None, 'tile'), may hold values from -6 to 6
Outputs:
- critical_density: float32 [4, 256, 2048], P(None, 'tile', 'member')
The draws below stay inside these ranges and needn't reach their ends.
All inputs are finite; a program needn't handle non-finite values.
Results may differ from the reference program's by a relative error of at most 0.0003.
Values may be sent and summed in bfloat16 or wider, within the bound.
A program may use at most 128 MiB of HBM per device.

```python
import jax
import jax.numpy as jnp
from jax import lax

LEVELS = 4
MEMBERS = 8
NLAT = 256
NLON = 2048


def draw_winds(key, part):
    key = jax.random.fold_in(key, 11)
    key_common, key_noise = jax.random.split(key, 2)
    common = jax.random.normal(key_common, (1, LEVELS, 2, NLAT, NLON), jnp.float32)
    noise = 0.8 * jax.random.normal(key_noise, (MEMBERS, LEVELS, 2, NLAT, NLON), jnp.float32)
    return jnp.clip(common + noise, -6.0, 6.0).astype(jnp.bfloat16)


def setup_inputs(seed: int = 0) -> dict:
    arg_keys = jax.random.split(jax.random.key(seed), 2)
    winds = draw_winds(jax.random.fold_in(arg_keys[1], 71), 0)
    return {"winds": winds}


ridge = 0.1

def member_moments(field):
    field = field.astype(jnp.float32)
    energy = 0.5 * (field[:, 0] * field[:, 0] + field[:, 1] * field[:, 1])
    grad_x = 0.5 * (jnp.roll(energy, -1, axis=2) - jnp.roll(energy, 1, axis=2))
    padded = jnp.pad(energy, ((0, 0), (1, 1), (0, 0)))
    grad_y = 0.5 * (padded[:, 2:] - padded[:, :-2])
    return jnp.stack([grad_x, grad_y, grad_x * grad_x, grad_x * grad_y, grad_y * grad_y])

def density(extended, count):
    rows = extended[:, :, :-2] + extended[:, :, 1:-1] + extended[:, :, 2:]
    pooled = rows[..., :-2] + rows[..., 1:-1] + rows[..., 2:]
    mean_x = pooled[0] / count
    mean_y = pooled[1] / count
    cxx = pooled[2] / count - mean_x * mean_x + ridge
    cxy = pooled[3] / count - mean_x * mean_y
    cyy = pooled[4] / count - mean_y * mean_y + ridge
    lower_a = jnp.sqrt(cxx)
    lower_b = cxy / lower_a
    lower_c = jnp.sqrt(cyy - lower_b * lower_b)
    first = -mean_x / lower_a
    second = (-mean_y - lower_b * first) / lower_c
    return jnp.exp(-0.5 * (first * first + second * second)) / (2.0 * jnp.pi * lower_a * lower_c)

def reference(winds):

    def accumulate(total, field):
        return (total + member_moments(field), None)
    start = jnp.zeros((5, LEVELS, NLAT, NLON), jnp.float32)
    moments, _ = lax.scan(accumulate, start, winds)
    wrapped = jnp.concatenate([moments[..., -1:], moments, moments[..., :1]], axis=3)
    extended = jnp.pad(wrapped, ((0, 0), (0, 0), (1, 1), (0, 0)))
    return density(extended, 9.0 * MEMBERS)
```

```python
import functools

import jax
import jax.numpy as jnp
from jax import lax
from jax.experimental import pallas as pl
from jax.experimental.pallas import tpu as pltpu
from jax.sharding import PartitionSpec as P

RIDGE = 0.1
MESH = pl.DeviceIdType.MESH
LANES = 128


def row_order(size, rows):
    out = lax.broadcasted_iota(jnp.int32, (size, size), 0)
    src = lax.broadcasted_iota(jnp.int32, (size, size), 1)
    wanted = ((out % 8) * 2 + (out // 8) % 2) * rows + out // 16
    return jnp.where(src == wanted, 1.0, 0.0).astype(jnp.bfloat16)


def pick(matrix, block):
    return jnp.dot(matrix, block, preferred_element_type=jnp.float32)


def west(x):
    return pltpu.roll(x, 1, 1)


def east(x):
    return pltpu.roll(x, x.shape[1] - 1, 1)


def fold(x, half):
    shape = (8, LANES)
    near = lax.broadcasted_iota(jnp.int32, shape, 1) < LANES // 2
    edge = x[:, 2 * half :]
    low = jnp.concatenate(
        [x[:, :half], jnp.where(near, x[:, half : half + LANES], edge)], axis=1
    )
    high = jnp.concatenate(
        [x[:, half : 2 * half], jnp.where(near, edge, x[:, half - LANES : half])], axis=1
    )
    upper = lax.broadcasted_iota(jnp.int32, low.shape, 0) < 4
    return jnp.where(upper, low, high) + pltpu.roll(jnp.where(upper, high, low), 4, 0)


def pool(x, half):
    return (x + west(x) + east(x))[:, :half]


def density(sum_x, sum_y, sum_xx, sum_xy, sum_yy, count):
    mean_x = sum_x * (0.25 / count)
    mean_y = sum_y * (0.25 / count)
    cxx = sum_xx * (0.0625 / count) - mean_x * mean_x + RIDGE
    cxy = sum_xy * (0.0625 / count) - mean_x * mean_y
    cyy = sum_yy * (0.0625 / count) - mean_y * mean_y + RIDGE
    inv_a = lax.rsqrt(cxx)
    lower_b = cxy * inv_a
    inv_c = lax.rsqrt(cyy - lower_b * lower_b)
    first = -mean_x * inv_a
    second = (-mean_y - lower_b * first) * inv_c
    return jnp.exp(-0.5 * (first * first + second * second)) * (inv_a * inv_c) * (0.5 / jnp.pi)


def kernel(
    n, tiles, rows, pairs, count,
    winds, out,
    own, slab, halo, edge_out, edge_in, energy, first, xx, xy, yy, ends_out, ends_in, dens,
    own_sem, here_sem, slab_send, slab_recv, halo_send, halo_recv,
    edge_send, edge_recv, ends_send, ends_recv,
):
    me, tile = lax.axis_index("member"), lax.axis_index("tile")
    lons = own.shape[1]
    width = lons // n
    half = width // 2
    size = 16 * rows
    has = (tile > 0, tile < tiles - 1)
    beside = (tile - 1, tile + 1)

    def peer(step):
        return lax.rem(me + step, n)

    def columns(start, length):
        return pl.ds(pl.multiple_of(start, LANES), length)

    load = pltpu.make_async_copy(winds, own, own_sem)
    load.start()
    here = pltpu.make_async_copy(
        winds.at[:, columns(me * width, width)], slab.at[0, :, pl.ds(0, width)], here_sem
    )
    here.start()

    barrier = pltpu.get_barrier_semaphore()
    for step in range(1, n):
        pl.semaphore_signal(
            barrier, inc=1, device_id={"member": peer(step), "tile": tile}, device_id_type=MESH
        )
    for side in range(2):
        @pl.when(has[side])
        def _():
            for step in range(n):
                pl.semaphore_signal(
                    barrier, inc=1, device_id={"member": peer(step), "tile": beside[side]},
                    device_id_type=MESH,
                )

    order = row_order(size, rows)
    ends = jnp.concatenate([order[:16], order[size - 16 :]], axis=0)
    load.wait()
    near = lax.broadcasted_iota(jnp.int32, (1, LANES), 1) < LANES // 2
    for q in range(pairs):
        packed = pick(ends, own[q * size : (q + 1) * size, :]).astype(jnp.bfloat16)
        for side in range(2):
            ends_rows = packed[side * 16 : (side + 1) * 16]
            edge_out[side, n, q * 16 : (q + 1) * 16, :lons] = ends_rows
    for step in range(n):
        to = peer(step)
        right = columns(lax.rem(to + 1, n) * width, LANES)
        left = columns(lax.rem(to + n - 1, n) * width + width - LANES, LANES)
        for side in range(2):
            edge_out[side, step, :, :width] = edge_out[side, n, :, columns(to * width, width)]
            edge_out[side, step, :, width : width + LANES] = jnp.where(
                near, edge_out[side, n, :, right], edge_out[side, n, :, left]
            )

    sides = jnp.where(has[0], 1, 0) + jnp.where(has[1], 1, 0)
    pl.semaphore_wait(barrier, n - 1 + n * sides)

    def edge_copy(side, step):
        return pltpu.make_async_remote_copy(
            src_ref=edge_out.at[side, step, :, pl.ds(0, width + LANES)],
            dst_ref=edge_in.at[1 - side, step],
            send_sem=edge_send.at[side, step],
            recv_sem=edge_recv.at[1 - side, step],
            device_id={"member": peer(step), "tile": beside[side]},
            device_id_type=MESH,
        )

    def edge_arrival(side, step):
        return pltpu.make_async_remote_copy(
            src_ref=edge_out.at[side, step, :, pl.ds(0, width + LANES)],
            dst_ref=edge_in.at[side, step],
            send_sem=edge_send.at[side, step],
            recv_sem=edge_recv.at[side, step],
            device_id={"member": peer(step), "tile": beside[side]},
            device_id_type=MESH,
        )

    for side in range(2):
        @pl.when(has[side])
        def _():
            for step in range(n):
                edge_copy(side, step).start()

    slab_copies, halo_copies = [], []
    for step in range(1, n):
        device = {"member": peer(step), "tile": tile}
        copy = pltpu.make_async_remote_copy(
            src_ref=winds.at[:, columns(peer(step) * width, width)],
            dst_ref=slab.at[step, :, pl.ds(0, width)],
            send_sem=slab_send.at[step], recv_sem=slab_recv.at[step],
            device_id=device, device_id_type=MESH,
        )
        copy.start()
        slab_copies.append(copy)

    for step in range(n):
        to = peer(step)
        right = columns(lax.rem(to + 1, n) * width, LANES)
        left = columns(lax.rem(to + n - 1, n) * width + width - LANES, LANES)
        tile_columns = jnp.where(near, own[:, right], own[:, left])
        if step == 0:
            slab[0, :, width:] = tile_columns
            continue
        halo[step - 1] = tile_columns
        copy = pltpu.make_async_remote_copy(
            src_ref=halo.at[step - 1],
            dst_ref=slab.at[step, :, pl.ds(width, LANES)],
            send_sem=halo_send.at[step], recv_sem=halo_recv.at[step],
            device_id={"member": to, "tile": tile}, device_id_type=MESH,
        )
        copy.start()
        halo_copies.append(copy)

    chunk = 3 * LANES if (width + LANES) % (3 * LANES) == 0 else LANES
    for step in range(n):
        if step == 0:
            here.wait()
        else:
            slab_copies[step - 1].wait_recv()
            halo_copies[step - 1].wait_recv()
        for q in range(pairs):
            for c in range(0, width + LANES, chunk):
                block = slab[step, q * size : (q + 1) * size, c : c + chunk]
                parts = pick(order, block).reshape(rows, 2, 8, chunk)
                energy[step * pairs + q, 1 : rows + 1, :, c : c + chunk] = (
                    parts[:, 0] * parts[:, 0] + parts[:, 1] * parts[:, 1]
                )

    groups = n * pairs

    def moments(i):
        total = sum_xx = sum_xy = sum_yy = None
        for p in range(groups):
            e = energy[p, i]
            gx = east(e) - west(e)
            gy = energy[p, i + 1] - energy[p, i - 1]
            terms = (e, gx * gx, gx * gy, gy * gy)
            if p == 0:
                total, sum_xx, sum_xy, sum_yy = terms
            else:
                total, sum_xx, sum_xy, sum_yy = (
                    total + terms[0], sum_xx + terms[1], sum_xy + terms[2], sum_yy + terms[3]
                )
        first[i] = fold(total, half)
        xx[i] = fold(sum_xx, half)
        xy[i] = fold(sum_xy, half)
        yy[i] = fold(sum_yy, half)

    def outer(i):
        total = sum_xx = None
        for p in range(groups):
            e = energy[p, i]
            gx = east(e) - west(e)
            total, sum_xx = (e, gx * gx) if p == 0 else (total + e, sum_xx + gx * gx)
        first[i] = fold(total, half)
        xx[i] = fold(sum_xx, half)

    pl.loop(2, rows)(moments)

    for side in range(2):
        row = 0 if side == 0 else rows + 1

        @pl.when(has[side])
        def _():
            for step in range(n):
                edge_arrival(side, step).wait_recv()
                for q in range(pairs):
                    parts = edge_in[side, step, q * 16 : (q + 1) * 16, :].astype(jnp.float32)
                    energy[step * pairs + q, row] = parts[:8] * parts[:8] + parts[8:] * parts[8:]

        @pl.when(jnp.logical_not(has[side]))
        def _():
            for p in range(groups):
                energy[p, row] = jnp.zeros_like(energy[p, row])
            ends_in[side] = jnp.zeros_like(ends_in[side])

    def ends_copy(side, landing):
        return pltpu.make_async_remote_copy(
            src_ref=ends_out.at[side],
            dst_ref=ends_in.at[landing],
            send_sem=ends_send.at[side],
            recv_sem=ends_recv.at[landing],
            device_id={"member": me, "tile": beside[side]},
            device_id_type=MESH,
        )

    for side in range(2):
        row, inner, beyond = (1, 2, 0) if side == 0 else (rows, rows - 1, rows + 1)
        moments(row)
        outer(beyond)
        ends_out[side, 0] = pool(first[row + 1] - first[row - 1], half)
        ends_out[side, 1] = pool(xy[row], half)
        ends_out[side, 2] = pool(yy[row], half)

        @pl.when(has[side])
        def _():
            ends_copy(side, 1 - side).start()

    def x_sums(i):
        s = first[i - 1] + first[i] + first[i + 1]
        s = s + west(s) + east(s)
        return (east(s) - west(s))[:, :half], pool(xx[i - 1] + xx[i] + xx[i + 1], half)

    def inside(i):
        sum_x, sum_xx = x_sums(i)
        sum_y = pool(first[i + 2] + first[i + 1] - first[i - 1] - first[i - 2], half)
        sum_xy = pool(xy[i - 1] + xy[i] + xy[i + 1], half)
        sum_yy = pool(yy[i - 1] + yy[i] + yy[i + 1], half)
        dens[i - 1] = density(sum_x, sum_y, sum_xx, sum_xy, sum_yy, count)

    pl.loop(2, rows)(inside)

    for side in range(2):
        row, inner = (1, 2) if side == 0 else (rows, rows - 1)
        sum_x, sum_xx = x_sums(row)

        @pl.when(has[side])
        def _():
            ends_copy(side, side).wait_recv()

        sum_y = ends_out[side, 0] + pool(first[inner + 1] - first[inner - 1], half) + ends_in[side, 0]
        sum_xy = ends_out[side, 1] + pool(xy[inner], half) + ends_in[side, 1]
        sum_yy = ends_out[side, 2] + pool(yy[inner], half) + ends_in[side, 2]
        dens[row - 1] = density(sum_x, sum_y, sum_xx, sum_xy, sum_yy, count)

    levels = out.shape[0]
    for r in range(0, rows, 8):
        turned = jnp.swapaxes(dens[r : r + 8], 0, 1)
        out[:, r : r + 8, :half] = turned[:levels]
        out[:, r : r + 8, half:] = turned[levels:]

    for copy in slab_copies + halo_copies:
        copy.wait_send()
    for side in range(2):
        @pl.when(has[side])
        def _():
            for step in range(n):
                edge_copy(side, step).wait_send()
            ends_copy(side, 1 - side).wait_send()


def per_device(n, tiles, winds):
    members, levels, parts, rows, lons = winds.shape
    width = lons // n
    half = width // 2
    pairs = members // 2
    size = 16 * rows
    assert levels == 4 and parts == 2 and members % 2 == 0 and rows % 8 == 0 and half % LANES == 0
    count = 9.0 * members * n
    groups = n * pairs
    dma = pltpu.SemaphoreType.DMA
    return pl.pallas_call(
        functools.partial(kernel, n, tiles, rows, pairs, count),
        out_shape=jax.ShapeDtypeStruct((levels, rows, width), jnp.float32),
        in_specs=[pl.BlockSpec(memory_space=pl.ANY)],
        out_specs=pl.BlockSpec(memory_space=pltpu.VMEM),
        scratch_shapes=[
            pltpu.VMEM((pairs * size, lons), jnp.bfloat16),
            pltpu.VMEM((n, pairs * size, width + LANES), jnp.bfloat16),
            pltpu.VMEM((max(n - 1, 1), pairs * size, LANES), jnp.bfloat16),
            pltpu.VMEM((2, n + 1, pairs * 16, max(lons, width + LANES)), jnp.bfloat16),
            pltpu.VMEM((2, n, pairs * 16, width + LANES), jnp.bfloat16),
            pltpu.VMEM((groups, rows + 2, 8, width + LANES), jnp.float32),
            pltpu.VMEM((rows + 2, 8, half + LANES), jnp.float32),
            pltpu.VMEM((rows + 2, 8, half + LANES), jnp.float32),
            pltpu.VMEM((rows + 2, 8, half + LANES), jnp.float32),
            pltpu.VMEM((rows + 2, 8, half + LANES), jnp.float32),
            pltpu.VMEM((2, 3, 8, half), jnp.float32),
            pltpu.VMEM((2, 3, 8, half), jnp.float32),
            pltpu.VMEM((rows, 8, half), jnp.float32),
            dma, dma, dma((n,)), dma((n,)), dma((n,)), dma((n,)),
            dma((2, n)), dma((2, n)), dma((2,)), dma((2,)),
        ],
        compiler_params=pltpu.CompilerParams(
            collective_id=0, has_side_effects=True, vmem_limit_bytes=48 * 2**20
        ),
    )(winds.reshape(pairs * size, lons))


def solution(mesh):
    return jax.shard_map(
        functools.partial(per_device, mesh.shape["member"], mesh.shape["tile"]),
        mesh=mesh,
        in_specs=(P("member", None, None, "tile", None),),
        out_specs=P(None, "tile", "member"),
        check_vma=False,
    )
```

```python
import functools

import jax
import jax.numpy as jnp
from jax import lax
from jax.experimental import pallas as pl
from jax.experimental.pallas import tpu as pltpu
from jax.sharding import PartitionSpec as P

RIDGE = 0.1
MESH = pl.DeviceIdType.MESH
LANES = 128


def row_order(size, rows):
    out = lax.broadcasted_iota(jnp.int32, (size, size), 0)
    src = lax.broadcasted_iota(jnp.int32, (size, size), 1)
    wanted = ((out % 8) * 2 + (out // 8) % 2) * rows + out // 16
    return jnp.where(src == wanted, 1.0, 0.0).astype(jnp.bfloat16)


def pick(matrix, block):
    return jnp.dot(matrix, block, preferred_element_type=jnp.float32)


def west(x):
    return pltpu.roll(x, 1, 1)


def east(x):
    return pltpu.roll(x, x.shape[1] - 1, 1)


def fold(x, half):
    shape = (8, LANES)
    near = lax.broadcasted_iota(jnp.int32, shape, 1) < LANES // 2
    edge = x[:, 2 * half :]
    low = jnp.concatenate(
        [x[:, :half], jnp.where(near, x[:, half : half + LANES], edge)], axis=1
    )
    high = jnp.concatenate(
        [x[:, half : 2 * half], jnp.where(near, edge, x[:, half - LANES : half])], axis=1
    )
    upper = lax.broadcasted_iota(jnp.int32, low.shape, 0) < 4
    return jnp.where(upper, low, high) + pltpu.roll(jnp.where(upper, high, low), 4, 0)


def pool(x, half):
    return (x + west(x) + east(x))[:, :half]


def density(sum_x, sum_y, sum_xx, sum_xy, sum_yy, count):
    mean_x = sum_x * (0.25 / count)
    mean_y = sum_y * (0.25 / count)
    cxx = sum_xx * (0.0625 / count) - mean_x * mean_x + RIDGE
    cxy = sum_xy * (0.0625 / count) - mean_x * mean_y
    cyy = sum_yy * (0.0625 / count) - mean_y * mean_y + RIDGE
    inv_a = lax.rsqrt(cxx)
    lower_b = cxy * inv_a
    inv_c = lax.rsqrt(cyy - lower_b * lower_b)
    first = -mean_x * inv_a
    second = (-mean_y - lower_b * first) * inv_c
    return jnp.exp(-0.5 * (first * first + second * second)) * (inv_a * inv_c) * (0.5 / jnp.pi)


def kernel(
    n, tiles, rows, pairs, count,
    winds, out,
    own, slab, halo, edge_all, edge_out, edge_in, energy, first, xx, xy, yy,
    early_out, early_in, late_out, late_in, dens,
    own_sem, here_sem, slab_send, slab_recv, halo_send, halo_recv,
    edge_send, edge_recv, early_send, early_recv, late_send, late_recv,
):
    me, tile = lax.axis_index("member"), lax.axis_index("tile")
    lons = own.shape[1]
    width = lons // n
    half = width // 2
    size = 16 * rows
    has = (tile > 0, tile < tiles - 1)
    beside = (tile - 1, tile + 1)

    def peer(step):
        return lax.rem(me + step, n)

    def columns(start, length):
        return pl.ds(pl.multiple_of(start, LANES), length)

    load = pltpu.make_async_copy(winds, own, own_sem)
    load.start()
    here = pltpu.make_async_copy(
        winds.at[:, columns(me * width, width)], slab.at[0, :, pl.ds(0, width)], here_sem
    )
    here.start()

    barrier = pltpu.get_barrier_semaphore()
    for step in range(1, n):
        pl.semaphore_signal(
            barrier, inc=1, device_id={"member": peer(step), "tile": tile}, device_id_type=MESH
        )
    for side in range(2):
        @pl.when(has[side])
        def _():
            for step in range(n):
                pl.semaphore_signal(
                    barrier, inc=1, device_id={"member": peer(step), "tile": beside[side]},
                    device_id_type=MESH,
                )

    order = row_order(size, rows)
    ends = jnp.concatenate([order[:16], order[size - 16 :]], axis=0)
    load.wait()
    near = lax.broadcasted_iota(jnp.int32, (1, LANES), 1) < LANES // 2
    lane = lax.broadcasted_iota(jnp.int32, (1, LANES), 1)
    for q in range(pairs):
        packed = pick(ends, own[q * size : (q + 1) * size, :]).astype(jnp.bfloat16)
        for side in range(2):
            edge_all[side, :, q * lons : (q + 1) * lons] = packed[side * 16 : (side + 1) * 16]
    for step in range(n):
        to = peer(step)
        right = lax.rem(to + 1, n) * width
        left = lax.rem(to + n - 1, n) * width + width - LANES
        for side in range(2):
            sides_tile = None
            for q in range(pairs):
                edge_out[side, step, :, q * width : (q + 1) * width] = edge_all[
                    side, :, columns(q * lons + to * width, width)
                ]
                after = edge_all[side, :, columns(q * lons + right, LANES)].astype(jnp.float32)
                before = edge_all[side, :, columns(q * lons + left, LANES)].astype(jnp.float32)
                if q == 0:
                    sides_tile = jnp.where(near, after, before)
                else:
                    after = pltpu.roll(after, 2 * q, 1)
                    before = pltpu.roll(before, LANES - 2 * q, 1)
                    sides_tile = jnp.where((lane >= 2 * q) & near, after, sides_tile)
                    sides_tile = jnp.where((lane < LANES - 2 * q) & ~near, before, sides_tile)
            edge_out[side, step, :, pairs * width :] = sides_tile.astype(jnp.bfloat16)

    sides = jnp.where(has[0], 1, 0) + jnp.where(has[1], 1, 0)
    pl.semaphore_wait(barrier, n - 1 + n * sides)

    def edge_copy(side, step):
        return pltpu.make_async_remote_copy(
            src_ref=edge_out.at[side, step],
            dst_ref=edge_in.at[1 - side, step],
            send_sem=edge_send.at[side, step],
            recv_sem=edge_recv.at[1 - side, step],
            device_id={"member": peer(step), "tile": beside[side]},
            device_id_type=MESH,
        )

    def edge_arrival(side, step):
        return pltpu.make_async_remote_copy(
            src_ref=edge_out.at[side, step],
            dst_ref=edge_in.at[side, step],
            send_sem=edge_send.at[side, step],
            recv_sem=edge_recv.at[side, step],
            device_id={"member": peer(step), "tile": beside[side]},
            device_id_type=MESH,
        )

    for side in range(2):
        @pl.when(has[side])
        def _():
            for step in range(n):
                edge_copy(side, step).start()

    slab_copies, halo_copies = [], []
    for step in range(1, n):
        device = {"member": peer(step), "tile": tile}
        copy = pltpu.make_async_remote_copy(
            src_ref=winds.at[:, columns(peer(step) * width, width)],
            dst_ref=slab.at[step, :, pl.ds(0, width)],
            send_sem=slab_send.at[step], recv_sem=slab_recv.at[step],
            device_id=device, device_id_type=MESH,
        )
        copy.start()
        slab_copies.append(copy)

    for step in range(n):
        to = peer(step)
        right = columns(lax.rem(to + 1, n) * width, LANES)
        left = columns(lax.rem(to + n - 1, n) * width + width - LANES, LANES)
        tile_columns = jnp.where(near, own[:, right], own[:, left])
        if step == 0:
            slab[0, :, width:] = tile_columns
            continue
        halo[step - 1] = tile_columns
        copy = pltpu.make_async_remote_copy(
            src_ref=halo.at[step - 1],
            dst_ref=slab.at[step, :, pl.ds(width, LANES)],
            send_sem=halo_send.at[step], recv_sem=halo_recv.at[step],
            device_id={"member": to, "tile": tile}, device_id_type=MESH,
        )
        copy.start()
        halo_copies.append(copy)

    chunk = 3 * LANES if (width + LANES) % (3 * LANES) == 0 else LANES
    for step in range(n):
        if step == 0:
            here.wait()
        else:
            slab_copies[step - 1].wait_recv()
            halo_copies[step - 1].wait_recv()
        for q in range(pairs):
            for c in range(0, width + LANES, chunk):
                block = slab[step, q * size : (q + 1) * size, c : c + chunk]
                parts = pick(order, block).reshape(rows, 2, 8, chunk)
                energy[step * pairs + q, 1 : rows + 1, :, c : c + chunk] = (
                    parts[:, 0] * parts[:, 0] + parts[:, 1] * parts[:, 1]
                )

    groups = n * pairs

    def total(term):
        value = term(0)
        for p in range(1, groups):
            value = jax.tree.map(jnp.add, value, term(p))
        return value

    def slope(e):
        return east(e) - west(e)

    def x_terms(p, i):
        e = energy[p, i]
        gx = slope(e)
        return e, gx * gx

    def x_moments(i):
        sums = total(lambda p: x_terms(p, i))
        first[i], xx[i] = (fold(x, half) for x in sums)

    def moments(i):
        def term(p):
            e = energy[p, i]
            gx = slope(e)
            gy = energy[p, i + 1] - energy[p, i - 1]
            return e, gx * gx, gx * gy, gy * gy

        first[i], xx[i], xy[i], yy[i] = (fold(x, half) for x in total(term))

    places = ((1, 2, 0, 1.0), (rows, rows - 1, rows + 1, -1.0))

    def remote(source, target, send, recv, side):
        return pltpu.make_async_remote_copy(
            src_ref=source, dst_ref=target, send_sem=send, recv_sem=recv,
            device_id={"member": me, "tile": beside[side]}, device_id_type=MESH,
        )

    def early_copy(side, landing):
        return remote(
            early_out.at[side], early_in.at[landing], early_send.at[side], early_recv.at[landing], side
        )

    def late_copy(side, landing):
        return remote(
            late_out.at[side], late_in.at[landing], late_send.at[side], late_recv.at[landing], side
        )

    for side in range(2):
        row, inner, beyond, sign = places[side]
        x_moments(row)
        moments(inner)
        cross = total(lambda p: slope(energy[p, row]) * energy[p, inner])
        early_out[side, 0] = pool(first[inner], half)
        early_out[side, 1] = pool(fold(cross, half), half)

        @pl.when(has[side])
        def _():
            early_copy(side, 1 - side).start()

    def x_sums(i):
        s = first[i - 1] + first[i] + first[i + 1]
        s = s + west(s) + east(s)
        return slope(s)[:, :half], pool(xx[i - 1] + xx[i] + xx[i + 1], half)

    def inside(i):
        sum_x, sum_xx = x_sums(i)
        sum_y = pool(first[i + 2] + first[i + 1] - first[i - 1] - first[i - 2], half)
        sum_xy = pool(xy[i - 1] + xy[i] + xy[i + 1], half)
        sum_yy = pool(yy[i - 1] + yy[i] + yy[i + 1], half)
        dens[i - 1] = density(sum_x, sum_y, sum_xx, sum_xy, sum_yy, count)

    pl.loop(3, rows - 1)(moments)
    pl.loop(3, rows - 1)(inside)

    for side in range(2):
        row, inner, beyond, sign = places[side]

        @pl.when(has[side])
        def _():
            for step in range(n):
                edge_arrival(side, step).wait_recv()
                tail = edge_in[side, step, :, pairs * width :].astype(jnp.float32)
                for q in range(pairs):
                    parts = edge_in[side, step, :, q * width : (q + 1) * width].astype(jnp.float32)
                    edge = tail if q == 0 else jnp.where(
                        near, pltpu.roll(tail, LANES - 2 * q, 1), pltpu.roll(tail, 2 * q, 1)
                    )
                    p = step * pairs + q
                    energy[p, beyond, :, :width] = parts[:8] * parts[:8] + parts[8:] * parts[8:]
                    energy[p, beyond, :, width:] = edge[:8] * edge[:8] + edge[8:] * edge[8:]

        @pl.when(jnp.logical_not(has[side]))
        def _():
            for p in range(groups):
                energy[p, beyond] = jnp.zeros_like(energy[p, beyond])
            early_in[side, 0] = pool(first[row], half)
            early_in[side, 1] = jnp.zeros_like(early_in[side, 1])
            late_in[side] = jnp.zeros_like(late_in[side])

        def gy_squared(p):
            gy = energy[p, inner] - energy[p, beyond]
            return gy * gy

        yy[row] = fold(total(gy_squared), half)
        late_out[side] = pool(yy[row], half)

        @pl.when(has[side])
        def _():
            late_copy(side, 1 - side).start()

    waiting = []
    for side in range(2):
        row, inner, beyond, sign = places[side]

        def edge_terms(p):
            e, other = energy[p, row], energy[p, beyond]
            gx, gx_other = slope(e), slope(other)
            gy = sign * (energy[p, inner] - other)
            return gx * gy, other, gx_other * gx_other, gx_other * e

        xy[row], first[beyond], xx[beyond], cross = (fold(x, half) for x in total(edge_terms))
        inside(inner)
        sum_x, sum_xx = x_sums(row)
        sum_y = pool(
            first[row + 1] - first[row - 1] + first[inner + 1] - first[inner - 1] + sign * first[row],
            half,
        )
        sum_xy = pool(xy[row] + xy[inner] + sign * cross, half)
        sum_yy = pool(yy[row] + yy[inner], half)
        waiting.append((sum_x, sum_y, sum_xx, sum_xy, sum_yy))

    levels = out.shape[0]
    for r in range(0, rows, 8):
        turned = jnp.swapaxes(dens[r : r + 8], 0, 1)
        out[:, r : r + 8, :half] = turned[:levels]
        out[:, r : r + 8, half:] = turned[levels:]

    for side in range(2):
        row, inner, beyond, sign = places[side]

        @pl.when(has[side])
        def _():
            early_copy(side, side).wait_recv()
            late_copy(side, side).wait_recv()

        sum_x, sum_y, sum_xx, sum_xy, sum_yy = waiting[side]
        sum_y = sum_y - sign * early_in[side, 0]
        sum_xy = sum_xy - sign * early_in[side, 1]
        sum_yy = sum_yy + late_in[side]
        edge_row = density(sum_x, sum_y, sum_xx, sum_xy, sum_yy, count)
        for level in range(levels):
            out[level, row - 1 : row, :half] = edge_row[level : level + 1]
            out[level, row - 1 : row, half:] = edge_row[levels + level : levels + level + 1]

    for copy in slab_copies + halo_copies:
        copy.wait_send()
    for side in range(2):
        @pl.when(has[side])
        def _():
            for step in range(n):
                edge_copy(side, step).wait_send()
            early_copy(side, 1 - side).wait_send()
            late_copy(side, 1 - side).wait_send()


def per_device(n, tiles, winds):
    members, levels, parts, rows, lons = winds.shape
    width = lons // n
    half = width // 2
    pairs = members // 2
    size = 16 * rows
    assert levels == 4 and parts == 2 and members % 2 == 0 and rows % 8 == 0 and half % LANES == 0
    count = 9.0 * members * n
    groups = n * pairs
    dma = pltpu.SemaphoreType.DMA
    return pl.pallas_call(
        functools.partial(kernel, n, tiles, rows, pairs, count),
        out_shape=jax.ShapeDtypeStruct((levels, rows, width), jnp.float32),
        in_specs=[pl.BlockSpec(memory_space=pl.ANY)],
        out_specs=pl.BlockSpec(memory_space=pltpu.VMEM),
        scratch_shapes=[
            pltpu.VMEM((pairs * size, lons), jnp.bfloat16),
            pltpu.VMEM((n, pairs * size, width + LANES), jnp.bfloat16),
            pltpu.VMEM((max(n - 1, 1), pairs * size, LANES), jnp.bfloat16),
            pltpu.VMEM((2, 16, pairs * lons), jnp.bfloat16),
            pltpu.VMEM((2, n, 16, pairs * width + LANES), jnp.bfloat16),
            pltpu.VMEM((2, n, 16, pairs * width + LANES), jnp.bfloat16),
            pltpu.VMEM((groups, rows + 2, 8, width + LANES), jnp.float32),
            pltpu.VMEM((rows + 2, 8, half + LANES), jnp.float32),
            pltpu.VMEM((rows + 2, 8, half + LANES), jnp.float32),
            pltpu.VMEM((rows + 2, 8, half + LANES), jnp.float32),
            pltpu.VMEM((rows + 2, 8, half + LANES), jnp.float32),
            pltpu.VMEM((2, 2, 8, half), jnp.float32),
            pltpu.VMEM((2, 2, 8, half), jnp.float32),
            pltpu.VMEM((2, 8, half), jnp.float32),
            pltpu.VMEM((2, 8, half), jnp.float32),
            pltpu.VMEM((rows, 8, half), jnp.float32),
            dma, dma, dma((n,)), dma((n,)), dma((n,)), dma((n,)),
            dma((2, n)), dma((2, n)), dma((2,)), dma((2,)), dma((2,)), dma((2,)),
        ],
        compiler_params=pltpu.CompilerParams(
            collective_id=0, has_side_effects=True, vmem_limit_bytes=60 * 2**20
        ),
    )(winds.reshape(pairs * size, lons))


def solution(mesh):
    return jax.shard_map(
        functools.partial(per_device, mesh.shape["member"], mesh.shape["tile"]),
        mesh=mesh,
        in_specs=(P("member", None, None, "tile", None),),
        out_specs=P(None, "tile", "member"),
        check_vma=False,
    )
```

```python
import functools

import jax
import jax.numpy as jnp
from jax import lax
from jax.experimental import pallas as pl
from jax.experimental.pallas import tpu as pltpu
from jax.sharding import PartitionSpec as P

RIDGE = 0.1
MESH = pl.DeviceIdType.MESH
LANES = 128


def row_order(size, rows):
    out = lax.broadcasted_iota(jnp.int32, (size, size), 0)
    src = lax.broadcasted_iota(jnp.int32, (size, size), 1)
    wanted = ((out % 8) * 2 + (out // 8) % 2) * rows + out // 16
    return jnp.where(src == wanted, 1.0, 0.0).astype(jnp.bfloat16)


def pick(matrix, block):
    return jnp.dot(matrix, block, preferred_element_type=jnp.float32)


def west(x):
    return pltpu.roll(x, 1, 1)


def east(x):
    return pltpu.roll(x, x.shape[1] - 1, 1)


def fold(x, half):
    shape = (8, LANES)
    near = lax.broadcasted_iota(jnp.int32, shape, 1) < LANES // 2
    edge = x[:, 2 * half :]
    low = jnp.concatenate(
        [x[:, :half], jnp.where(near, x[:, half : half + LANES], edge)], axis=1
    )
    high = jnp.concatenate(
        [x[:, half : 2 * half], jnp.where(near, edge, x[:, half - LANES : half])], axis=1
    )
    upper = lax.broadcasted_iota(jnp.int32, low.shape, 0) < 4
    return jnp.where(upper, low, high) + pltpu.roll(jnp.where(upper, high, low), 4, 0)


def pool(x, half):
    return (x + west(x) + east(x))[:, :half]


def density(sum_x, sum_y, sum_xx, sum_xy, sum_yy, count):
    mean_x = sum_x * (0.25 / count)
    mean_y = sum_y * (0.25 / count)
    cxx = sum_xx * (0.0625 / count) - mean_x * mean_x + RIDGE
    cxy = sum_xy * (0.0625 / count) - mean_x * mean_y
    cyy = sum_yy * (0.0625 / count) - mean_y * mean_y + RIDGE
    inv_a = lax.rsqrt(cxx)
    lower_b = cxy * inv_a
    inv_c = lax.rsqrt(cyy - lower_b * lower_b)
    first = -mean_x * inv_a
    second = (-mean_y - lower_b * first) * inv_c
    return jnp.exp(-0.5 * (first * first + second * second)) * (inv_a * inv_c) * (0.5 / jnp.pi)


def kernel(
    n, tiles, rows, pairs, count,
    winds, out,
    own, slab, halo_out, halo_in, edge_all, edge_out, edge_in, energy, first, xx, xy, yy,
    early_out, early_in, late_out, late_in, dens,
    own_sem, slab_send, slab_recv, halo_send, halo_recv,
    edge_send, edge_recv, early_send, early_recv, late_send, late_recv,
):
    me, tile = lax.axis_index("member"), lax.axis_index("tile")
    lons = own.shape[1]
    width = lons // n
    half = width // 2
    size = 16 * rows
    has = (tile > 0, tile < tiles - 1)
    beside = (tile - 1, tile + 1)

    def peer(step):
        return lax.rem(me + step, n)

    def columns(start, length):
        return pl.ds(pl.multiple_of(start, LANES), length)

    load = pltpu.make_async_copy(winds, own, own_sem)
    load.start()

    barrier = pltpu.get_barrier_semaphore()
    for step in range(1, n):
        pl.semaphore_signal(
            barrier, inc=1, device_id={"member": peer(step), "tile": tile}, device_id_type=MESH
        )
    for side in range(2):
        @pl.when(has[side])
        def _():
            for step in range(n):
                pl.semaphore_signal(
                    barrier, inc=1, device_id={"member": peer(step), "tile": beside[side]},
                    device_id_type=MESH,
                )

    order = row_order(size, rows)
    ends = jnp.concatenate([order[:16], order[size - 16 :]], axis=0)
    load.wait()
    near = lax.broadcasted_iota(jnp.int32, (1, LANES), 1) < LANES // 2
    lane = lax.broadcasted_iota(jnp.int32, (1, LANES), 1)
    for q in range(pairs):
        packed = pick(ends, own[q * size : (q + 1) * size, :]).astype(jnp.bfloat16)
        for side in range(2):
            edge_all[side, :, q * lons : (q + 1) * lons] = packed[side * 16 : (side + 1) * 16]
    for step in range(n):
        to = peer(step)
        right = lax.rem(to + 1, n) * width
        left = lax.rem(to + n - 1, n) * width + width - LANES
        for side in range(2):
            sides_tile = None
            for q in range(pairs):
                edge_out[side, step, :, q * width : (q + 1) * width] = edge_all[
                    side, :, columns(q * lons + to * width, width)
                ]
                after = edge_all[side, :, columns(q * lons + right, LANES)].astype(jnp.float32)
                before = edge_all[side, :, columns(q * lons + left, LANES)].astype(jnp.float32)
                if q == 0:
                    sides_tile = jnp.where(near, after, before)
                else:
                    after = pltpu.roll(after, 2 * q, 1)
                    before = pltpu.roll(before, LANES - 2 * q, 1)
                    sides_tile = jnp.where((lane >= 2 * q) & near, after, sides_tile)
                    sides_tile = jnp.where((lane < LANES - 2 * q) & ~near, before, sides_tile)
            edge_out[side, step, :, pairs * width :] = sides_tile.astype(jnp.bfloat16)

    for step in range(n):
        to = peer(step)
        right = columns(lax.rem(to + 1, n) * width, LANES)
        left = columns(lax.rem(to + n - 1, n) * width + width - LANES, LANES)
        halo_out[step] = jnp.where(near, own[:, right], own[:, left])

    def energies(step, main, halo):
        for q in range(pairs):
            here = slice(q * size, (q + 1) * size)
            for c in range(0, width + LANES, 2 * LANES):
                chunk = 2 * LANES if c < width else LANES
                block = main(here, c, chunk) if c < width else halo[here, :]
                parts = pick(order, block).reshape(rows, 2, 8, chunk)
                energy[step * pairs + q, 1 : rows + 1, :, c : c + chunk] = (
                    parts[:, 0] * parts[:, 0] + parts[:, 1] * parts[:, 1]
                )

    energies(0, lambda here, c, chunk: own[here, columns(me * width + c, chunk)], halo_out.at[0])

    sides = jnp.where(has[0], 1, 0) + jnp.where(has[1], 1, 0)
    pl.semaphore_wait(barrier, n - 1 + n * sides)

    def edge_copy(side, step):
        return pltpu.make_async_remote_copy(
            src_ref=edge_out.at[side, step],
            dst_ref=edge_in.at[1 - side, step],
            send_sem=edge_send.at[side, step],
            recv_sem=edge_recv.at[1 - side, step],
            device_id={"member": peer(step), "tile": beside[side]},
            device_id_type=MESH,
        )

    def edge_arrival(side, step):
        return pltpu.make_async_remote_copy(
            src_ref=edge_out.at[side, step],
            dst_ref=edge_in.at[side, step],
            send_sem=edge_send.at[side, step],
            recv_sem=edge_recv.at[side, step],
            device_id={"member": peer(step), "tile": beside[side]},
            device_id_type=MESH,
        )

    for side in range(2):
        @pl.when(has[side])
        def _():
            for step in range(n):
                edge_copy(side, step).start()

    slab_copies, halo_copies = [], []
    for step in range(1, n):
        device = {"member": peer(step), "tile": tile}
        copy = pltpu.make_async_remote_copy(
            src_ref=winds.at[:, columns(peer(step) * width, width)],
            dst_ref=slab.at[step - 1],
            send_sem=slab_send.at[step], recv_sem=slab_recv.at[step],
            device_id=device, device_id_type=MESH,
        )
        copy.start()
        slab_copies.append(copy)
        copy = pltpu.make_async_remote_copy(
            src_ref=halo_out.at[step],
            dst_ref=halo_in.at[step - 1],
            send_sem=halo_send.at[step], recv_sem=halo_recv.at[step],
            device_id=device, device_id_type=MESH,
        )
        copy.start()
        halo_copies.append(copy)

    groups = n * pairs

    def total(term, start=0, stop=groups):
        value = term(start)
        for p in range(start + 1, stop):
            value = jax.tree.map(jnp.add, value, term(p))
        return value

    def slope(e):
        return east(e) - west(e)

    def x_terms(p, i):
        e = energy[p, i]
        gx = slope(e)
        return e, gx * gx

    def terms(p, i):
        e = energy[p, i]
        gx = slope(e)
        gy = energy[p, i + 1] - energy[p, i - 1]
        return e, gx * gx, gx * gy, gy * gy

    def put(targets, i, sums, more):
        for target, x in zip(targets, sums):
            x = fold(x, half)
            target[i] = target[i] + x if more else x

    def x_moments(i, start, stop):
        put((first, xx), i, total(lambda p: x_terms(p, i), start, stop), start > 0)

    def moments(i, start, stop):
        put((first, xx, xy, yy), i, total(lambda p: terms(p, i), start, stop), start > 0)

    def band(start, stop):
        for i in (1, rows):
            x_moments(i, start, stop)
        for i in (2, rows - 1):
            moments(i, start, stop)
        pl.loop(3, rows - 1, unroll=4)(lambda i: moments(i, start, stop))

    band(0, pairs)
    for step in range(1, n):
        slab_copies[step - 1].wait_recv()
        halo_copies[step - 1].wait_recv()
        energies(
            step,
            lambda here, c, chunk: slab[step - 1, here, c : c + chunk],
            halo_in.at[step - 1],
        )
    if n > 1:
        band(pairs, groups)

    places = ((1, 2, 0, 1.0), (rows, rows - 1, rows + 1, -1.0))

    def remote(source, target, send, recv, side):
        return pltpu.make_async_remote_copy(
            src_ref=source, dst_ref=target, send_sem=send, recv_sem=recv,
            device_id={"member": me, "tile": beside[side]}, device_id_type=MESH,
        )

    def early_copy(side, landing):
        return remote(
            early_out.at[side], early_in.at[landing], early_send.at[side], early_recv.at[landing], side
        )

    def late_copy(side, landing):
        return remote(
            late_out.at[side], late_in.at[landing], late_send.at[side], late_recv.at[landing], side
        )

    for side in range(2):
        row, inner, beyond, sign = places[side]
        cross = total(lambda p: slope(energy[p, row]) * energy[p, inner])
        early_out[side, 0] = pool(first[inner], half)
        early_out[side, 1] = pool(fold(cross, half), half)

        @pl.when(has[side])
        def _():
            early_copy(side, 1 - side).start()

    def x_sums(i):
        s = first[i - 1] + first[i] + first[i + 1]
        s = s + west(s) + east(s)
        return slope(s)[:, :half], pool(xx[i - 1] + xx[i] + xx[i + 1], half)

    def inside(i):
        sum_x, sum_xx = x_sums(i)
        sum_y = pool(first[i + 2] + first[i + 1] - first[i - 1] - first[i - 2], half)
        sum_xy = pool(xy[i - 1] + xy[i] + xy[i + 1], half)
        sum_yy = pool(yy[i - 1] + yy[i] + yy[i + 1], half)
        dens[i - 1] = density(sum_x, sum_y, sum_xx, sum_xy, sum_yy, count)

    pl.loop(3, rows - 1, unroll=4)(inside)

    for side in range(2):
        row, inner, beyond, sign = places[side]

        @pl.when(has[side])
        def _():
            for step in range(n):
                edge_arrival(side, step).wait_recv()
                tail = edge_in[side, step, :, pairs * width :].astype(jnp.float32)
                for q in range(pairs):
                    parts = edge_in[side, step, :, q * width : (q + 1) * width].astype(jnp.float32)
                    edge = tail if q == 0 else jnp.where(
                        near, pltpu.roll(tail, LANES - 2 * q, 1), pltpu.roll(tail, 2 * q, 1)
                    )
                    p = step * pairs + q
                    energy[p, beyond, :, :width] = parts[:8] * parts[:8] + parts[8:] * parts[8:]
                    energy[p, beyond, :, width:] = edge[:8] * edge[:8] + edge[8:] * edge[8:]

        @pl.when(jnp.logical_not(has[side]))
        def _():
            for p in range(groups):
                energy[p, beyond] = jnp.zeros_like(energy[p, beyond])
            early_in[side, 0] = pool(first[row], half)
            early_in[side, 1] = jnp.zeros_like(early_in[side, 1])
            late_in[side] = jnp.zeros_like(late_in[side])

        def gy_squared(p):
            gy = energy[p, inner] - energy[p, beyond]
            return gy * gy

        yy[row] = fold(total(gy_squared), half)
        late_out[side] = pool(yy[row], half)

        @pl.when(has[side])
        def _():
            late_copy(side, 1 - side).start()

    waiting = []
    for side in range(2):
        row, inner, beyond, sign = places[side]

        def edge_terms(p):
            e, other = energy[p, row], energy[p, beyond]
            gx, gx_other = slope(e), slope(other)
            gy = sign * (energy[p, inner] - other)
            return gx * gy, other, gx_other * gx_other, gx_other * e

        xy[row], first[beyond], xx[beyond], cross = (fold(x, half) for x in total(edge_terms))
        inside(inner)
        sum_x, sum_xx = x_sums(row)
        sum_y = pool(
            first[row + 1] - first[row - 1] + first[inner + 1] - first[inner - 1] + sign * first[row],
            half,
        )
        sum_xy = pool(xy[row] + xy[inner] + sign * cross, half)
        sum_yy = pool(yy[row] + yy[inner], half)
        waiting.append((sum_x, sum_y, sum_xx, sum_xy, sum_yy))

    levels = out.shape[0]
    for r in range(0, rows, 8):
        turned = jnp.swapaxes(dens[r : r + 8], 0, 1)
        out[:, r : r + 8, :half] = turned[:levels]
        out[:, r : r + 8, half:] = turned[levels:]

    for side in range(2):
        row, inner, beyond, sign = places[side]

        @pl.when(has[side])
        def _():
            early_copy(side, side).wait_recv()
            late_copy(side, side).wait_recv()

        sum_x, sum_y, sum_xx, sum_xy, sum_yy = waiting[side]
        sum_y = sum_y - sign * early_in[side, 0]
        sum_xy = sum_xy - sign * early_in[side, 1]
        sum_yy = sum_yy + late_in[side]
        edge_row = density(sum_x, sum_y, sum_xx, sum_xy, sum_yy, count)
        for level in range(levels):
            out[level, row - 1 : row, :half] = edge_row[level : level + 1]
            out[level, row - 1 : row, half:] = edge_row[levels + level : levels + level + 1]

    for copy in slab_copies + halo_copies:
        copy.wait_send()
    for side in range(2):
        @pl.when(has[side])
        def _():
            for step in range(n):
                edge_copy(side, step).wait_send()
            early_copy(side, 1 - side).wait_send()
            late_copy(side, 1 - side).wait_send()


def per_device(n, tiles, winds):
    members, levels, parts, rows, lons = winds.shape
    width = lons // n
    half = width // 2
    pairs = members // 2
    size = 16 * rows
    assert levels == 4 and parts == 2 and members % 2 == 0 and rows % 8 == 0 and half % LANES == 0
    count = 9.0 * members * n
    groups = n * pairs
    dma = pltpu.SemaphoreType.DMA
    return pl.pallas_call(
        functools.partial(kernel, n, tiles, rows, pairs, count),
        out_shape=jax.ShapeDtypeStruct((levels, rows, width), jnp.float32),
        in_specs=[pl.BlockSpec(memory_space=pl.ANY)],
        out_specs=pl.BlockSpec(memory_space=pltpu.VMEM),
        scratch_shapes=[
            pltpu.VMEM((pairs * size, lons), jnp.bfloat16),
            pltpu.VMEM((max(n - 1, 1), pairs * size, width), jnp.bfloat16),
            pltpu.VMEM((n, pairs * size, LANES), jnp.bfloat16),
            pltpu.VMEM((max(n - 1, 1), pairs * size, LANES), jnp.bfloat16),
            pltpu.VMEM((2, 16, pairs * lons), jnp.bfloat16),
            pltpu.VMEM((2, n, 16, pairs * width + LANES), jnp.bfloat16),
            pltpu.VMEM((2, n, 16, pairs * width + LANES), jnp.bfloat16),
            pltpu.VMEM((groups, rows + 2, 8, width + LANES), jnp.float32),
            pltpu.VMEM((rows + 2, 8, half + LANES), jnp.float32),
            pltpu.VMEM((rows + 2, 8, half + LANES), jnp.float32),
            pltpu.VMEM((rows + 2, 8, half + LANES), jnp.float32),
            pltpu.VMEM((rows + 2, 8, half + LANES), jnp.float32),
            pltpu.VMEM((2, 2, 8, half), jnp.float32),
            pltpu.VMEM((2, 2, 8, half), jnp.float32),
            pltpu.VMEM((2, 8, half), jnp.float32),
            pltpu.VMEM((2, 8, half), jnp.float32),
            pltpu.VMEM((rows, 8, half), jnp.float32),
            dma, dma((n,)), dma((n,)), dma((n,)), dma((n,)),
            dma((2, n)), dma((2, n)), dma((2,)), dma((2,)), dma((2,)), dma((2,)),
        ],
        compiler_params=pltpu.CompilerParams(
            collective_id=0, has_side_effects=True, vmem_limit_bytes=60 * 2**20
        ),
    )(winds.reshape(pairs * size, lons))


def solution(mesh):
    return jax.shard_map(
        functools.partial(per_device, mesh.shape["member"], mesh.shape["tile"]),
        mesh=mesh,
        in_specs=(P("member", None, None, "tile", None),),
        out_specs=P(None, "tile", "member"),
        check_vma=False,
    )
```

```python
import functools

import jax
import jax.numpy as jnp
from jax import lax
from jax.experimental import pallas as pl
from jax.experimental.pallas import tpu as pltpu
from jax.sharding import PartitionSpec as P

RIDGE = 0.1
MESH = pl.DeviceIdType.MESH
LANES = 128


def row_order(size, rows):
    out = lax.broadcasted_iota(jnp.int32, (size, size), 0)
    src = lax.broadcasted_iota(jnp.int32, (size, size), 1)
    wanted = ((out % 8) * 2 + (out // 8) % 2) * rows + out // 16
    return jnp.where(src == wanted, 1.0, 0.0).astype(jnp.bfloat16)


def pick(matrix, block):
    return jnp.dot(matrix, block, preferred_element_type=jnp.float32)


def west(x):
    return pltpu.roll(x, 1, 1)


def east(x):
    return pltpu.roll(x, x.shape[1] - 1, 1)


def fold(x, half):
    shape = (8, LANES)
    near = lax.broadcasted_iota(jnp.int32, shape, 1) < LANES // 2
    edge = x[:, 2 * half :]
    low = jnp.concatenate(
        [x[:, :half], jnp.where(near, x[:, half : half + LANES], edge)], axis=1
    )
    high = jnp.concatenate(
        [x[:, half : 2 * half], jnp.where(near, edge, x[:, half - LANES : half])], axis=1
    )
    upper = lax.broadcasted_iota(jnp.int32, low.shape, 0) < 4
    return jnp.where(upper, low, high) + pltpu.roll(jnp.where(upper, high, low), 4, 0)


def pool(x, half):
    return (x + west(x) + east(x))[:, :half]


def density(sum_x, sum_y, sum_xx, sum_xy, sum_yy, count):
    mean_x = sum_x * (0.25 / count)
    mean_y = sum_y * (0.25 / count)
    cxx = sum_xx * (0.0625 / count) - mean_x * mean_x + RIDGE
    cxy = sum_xy * (0.0625 / count) - mean_x * mean_y
    cyy = sum_yy * (0.0625 / count) - mean_y * mean_y + RIDGE
    inv_a = lax.rsqrt(cxx)
    lower_b = cxy * inv_a
    inv_c = lax.rsqrt(cyy - lower_b * lower_b)
    first = -mean_x * inv_a
    second = (-mean_y - lower_b * first) * inv_c
    return jnp.exp(-0.5 * (first * first + second * second)) * (inv_a * inv_c) * (0.5 / jnp.pi)


def kernel(
    n, tiles, rows, pairs, count,
    winds, out,
    own, slab, halo_out, halo_in, edge_all, edge_out, edge_in, energy, first, xx, xy, yy,
    early_out, early_in, late_out, late_in, dens,
    own_sem, slab_send, slab_recv, halo_send, halo_recv,
    edge_send, edge_recv, early_send, early_recv, late_send, late_recv,
):
    me, tile = lax.axis_index("member"), lax.axis_index("tile")
    lons = own.shape[1]
    width = lons // n
    half = width // 2
    size = 16 * rows
    has = (tile > 0, tile < tiles - 1)
    beside = (tile - 1, tile + 1)

    def peer(step):
        return lax.rem(me + step, n)

    def columns(start, length):
        return pl.ds(pl.multiple_of(start, LANES), length)

    share = pairs * size // 8
    loads = []
    for k in range(8):
        piece = pl.ds(k * share, share)
        load = pltpu.make_async_copy(winds.at[piece], own.at[piece], own_sem.at[k])
        load.start()
        loads.append(load)

    barrier = pltpu.get_barrier_semaphore()
    for step in range(1, n):
        pl.semaphore_signal(
            barrier, inc=1, device_id={"member": peer(step), "tile": tile}, device_id_type=MESH
        )
    for side in range(2):
        @pl.when(has[side])
        def _():
            for step in range(n):
                pl.semaphore_signal(
                    barrier, inc=1, device_id={"member": peer(step), "tile": beside[side]},
                    device_id_type=MESH,
                )

    order = row_order(size, rows)
    ends = jnp.concatenate([order[:16], order[size - 16 :]], axis=0)
    for load in loads:
        load.wait()
    near = lax.broadcasted_iota(jnp.int32, (1, LANES), 1) < LANES // 2
    lane = lax.broadcasted_iota(jnp.int32, (1, LANES), 1)
    for q in range(pairs):
        packed = pick(ends, own[q * size : (q + 1) * size, :]).astype(jnp.bfloat16)
        for side in range(2):
            edge_all[side, :, q * lons : (q + 1) * lons] = packed[side * 16 : (side + 1) * 16]
    for step in range(n):
        to = peer(step)
        right = lax.rem(to + 1, n) * width
        left = lax.rem(to + n - 1, n) * width + width - LANES
        for side in range(2):
            sides_tile = None
            for q in range(pairs):
                edge_out[side, step, :, q * width : (q + 1) * width] = edge_all[
                    side, :, columns(q * lons + to * width, width)
                ]
                after = edge_all[side, :, columns(q * lons + right, LANES)].astype(jnp.float32)
                before = edge_all[side, :, columns(q * lons + left, LANES)].astype(jnp.float32)
                if q == 0:
                    sides_tile = jnp.where(near, after, before)
                else:
                    after = pltpu.roll(after, 2 * q, 1)
                    before = pltpu.roll(before, LANES - 2 * q, 1)
                    sides_tile = jnp.where((lane >= 2 * q) & near, after, sides_tile)
                    sides_tile = jnp.where((lane < LANES - 2 * q) & ~near, before, sides_tile)
            edge_out[side, step, :, pairs * width :] = sides_tile.astype(jnp.bfloat16)

    def energies(step, main, halo):
        for q in range(pairs):
            here = slice(q * size, (q + 1) * size)
            for c in range(0, width + LANES, 2 * LANES):
                chunk = 2 * LANES if c < width else LANES
                block = main(here, c, chunk) if c < width else halo[here, :]
                parts = pick(order, block).reshape(rows, 2, 8, chunk)
                energy[step * pairs + q, 1 : rows + 1, :, c : c + chunk] = (
                    parts[:, 0] * parts[:, 0] + parts[:, 1] * parts[:, 1]
                )

    sides = jnp.where(has[0], 1, 0) + jnp.where(has[1], 1, 0)
    pl.semaphore_wait(barrier, n - 1 + n * sides)

    def edge_copy(side, step):
        return pltpu.make_async_remote_copy(
            src_ref=edge_out.at[side, step],
            dst_ref=edge_in.at[1 - side, step],
            send_sem=edge_send.at[side, step],
            recv_sem=edge_recv.at[1 - side, step],
            device_id={"member": peer(step), "tile": beside[side]},
            device_id_type=MESH,
        )

    def edge_arrival(side, step):
        return pltpu.make_async_remote_copy(
            src_ref=edge_out.at[side, step],
            dst_ref=edge_in.at[side, step],
            send_sem=edge_send.at[side, step],
            recv_sem=edge_recv.at[side, step],
            device_id={"member": peer(step), "tile": beside[side]},
            device_id_type=MESH,
        )

    for side in range(2):
        @pl.when(has[side])
        def _():
            for step in range(n):
                edge_copy(side, step).start()

    for step in range(n):
        to = peer(step)
        right = columns(lax.rem(to + 1, n) * width, LANES)
        left = columns(lax.rem(to + n - 1, n) * width + width - LANES, LANES)
        halo_out[step] = jnp.where(near, own[:, right], own[:, left])

    slab_copies, halo_copies = [], []
    for step in range(1, n):
        device = {"member": peer(step), "tile": tile}
        copy = pltpu.make_async_remote_copy(
            src_ref=winds.at[:, columns(peer(step) * width, width)],
            dst_ref=slab.at[step - 1],
            send_sem=slab_send.at[step], recv_sem=slab_recv.at[step],
            device_id=device, device_id_type=MESH,
        )
        copy.start()
        slab_copies.append(copy)
        copy = pltpu.make_async_remote_copy(
            src_ref=halo_out.at[step],
            dst_ref=halo_in.at[step - 1],
            send_sem=halo_send.at[step], recv_sem=halo_recv.at[step],
            device_id=device, device_id_type=MESH,
        )
        copy.start()
        halo_copies.append(copy)

    groups = n * pairs

    def total(term, start=0, stop=groups):
        value = term(start)
        for p in range(start + 1, stop):
            value = jax.tree.map(jnp.add, value, term(p))
        return value

    def slope(e):
        return east(e) - west(e)

    def x_terms(p, i):
        e = energy[p, i]
        gx = slope(e)
        return e, gx * gx

    def terms(p, i):
        e = energy[p, i]
        gx = slope(e)
        gy = energy[p, i + 1] - energy[p, i - 1]
        return e, gx * gx, gx * gy, gy * gy

    def put(targets, i, sums, more):
        for target, x in zip(targets, sums):
            x = fold(x, half)
            target[i] = target[i] + x if more else x

    def x_moments(i, start, stop):
        put((first, xx), i, total(lambda p: x_terms(p, i), start, stop), start > 0)

    def moments(i, start, stop):
        put((first, xx, xy, yy), i, total(lambda p: terms(p, i), start, stop), start > 0)

    def band(start, stop):
        for i in (1, rows):
            x_moments(i, start, stop)
        for i in (2, rows - 1):
            moments(i, start, stop)
        pl.loop(3, rows - 1, unroll=4)(lambda i: moments(i, start, stop))

    energies(0, lambda here, c, chunk: own[here, columns(me * width + c, chunk)], halo_out.at[0])
    band(0, pairs)
    for step in range(1, n):
        slab_copies[step - 1].wait_recv()
        halo_copies[step - 1].wait_recv()
        energies(
            step,
            lambda here, c, chunk: slab[step - 1, here, c : c + chunk],
            halo_in.at[step - 1],
        )
    if n > 1:
        band(pairs, groups)

    places = ((1, 2, 0, 1.0), (rows, rows - 1, rows + 1, -1.0))

    def remote(source, target, send, recv, side):
        return pltpu.make_async_remote_copy(
            src_ref=source, dst_ref=target, send_sem=send, recv_sem=recv,
            device_id={"member": me, "tile": beside[side]}, device_id_type=MESH,
        )

    def early_copy(side, landing):
        return remote(
            early_out.at[side], early_in.at[landing], early_send.at[side], early_recv.at[landing], side
        )

    def late_copy(side, landing):
        return remote(
            late_out.at[side], late_in.at[landing], late_send.at[side], late_recv.at[landing], side
        )

    for side in range(2):
        row, inner, beyond, sign = places[side]
        cross = total(lambda p: slope(energy[p, row]) * energy[p, inner])
        early_out[side, 0] = pool(first[inner], half)
        early_out[side, 1] = pool(fold(cross, half), half)

        @pl.when(has[side])
        def _():
            early_copy(side, 1 - side).start()

    def x_sums(i):
        s = first[i - 1] + first[i] + first[i + 1]
        s = s + west(s) + east(s)
        return slope(s)[:, :half], pool(xx[i - 1] + xx[i] + xx[i + 1], half)

    def inside(i):
        sum_x, sum_xx = x_sums(i)
        sum_y = pool(first[i + 2] + first[i + 1] - first[i - 1] - first[i - 2], half)
        sum_xy = pool(xy[i - 1] + xy[i] + xy[i + 1], half)
        sum_yy = pool(yy[i - 1] + yy[i] + yy[i + 1], half)
        dens[i - 1] = density(sum_x, sum_y, sum_xx, sum_xy, sum_yy, count)

    pl.loop(3, rows - 1, unroll=4)(inside)

    for side in range(2):
        row, inner, beyond, sign = places[side]

        @pl.when(has[side])
        def _():
            main = tail = None
            for step in range(n):
                edge_arrival(side, step).wait_recv()
                sides_tile = edge_in[side, step, :, pairs * width :].astype(jnp.float32)
                for q in range(pairs):
                    p = step * pairs + q
                    parts = edge_in[side, step, :, q * width : (q + 1) * width].astype(jnp.float32)
                    edge = sides_tile if q == 0 else jnp.where(
                        near,
                        pltpu.roll(sides_tile, LANES - 2 * q, 1),
                        pltpu.roll(sides_tile, 2 * q, 1),
                    )
                    e = parts[:8] * parts[:8] + parts[8:] * parts[8:]
                    e_tail = edge[:8] * edge[:8] + edge[8:] * edge[8:]
                    energy[p, beyond, :, :width] = e
                    energy[p, beyond, :, width:] = e_tail
                    gy = energy[p, inner, :, :width] - e
                    gy_tail = energy[p, inner, :, width:] - e_tail
                    main = gy * gy if p == 0 else main + gy * gy
                    tail = gy_tail * gy_tail if p == 0 else tail + gy_tail * gy_tail
            folded = fold(jnp.concatenate([main, tail], axis=1), half)
            late_out[side] = pool(folded, half)
            late_copy(side, 1 - side).start()
            yy[row] = folded

        @pl.when(jnp.logical_not(has[side]))
        def _():
            for p in range(groups):
                energy[p, beyond] = jnp.zeros_like(energy[p, beyond])
            early_in[side, 0] = pool(first[row], half)
            early_in[side, 1] = jnp.zeros_like(early_in[side, 1])
            late_in[side] = jnp.zeros_like(late_in[side])
            folded = fold(total(lambda p: energy[p, inner] * energy[p, inner]), half)
            late_out[side] = pool(folded, half)
            yy[row] = folded

    waiting = []
    for side in range(2):
        row, inner, beyond, sign = places[side]

        def edge_terms(p):
            e, other = energy[p, row], energy[p, beyond]
            gx, gx_other = slope(e), slope(other)
            gy = sign * (energy[p, inner] - other)
            return gx * gy, other, gx_other * gx_other, gx_other * e

        xy[row], first[beyond], xx[beyond], cross = (fold(x, half) for x in total(edge_terms))
        inside(inner)
        sum_x, sum_xx = x_sums(row)
        sum_y = pool(
            first[row + 1] - first[row - 1] + first[inner + 1] - first[inner - 1] + sign * first[row],
            half,
        )
        sum_xy = pool(xy[row] + xy[inner] + sign * cross, half)
        sum_yy = pool(yy[row] + yy[inner], half)
        waiting.append((sum_x, sum_y, sum_xx, sum_xy, sum_yy))

    levels = out.shape[0]
    for r in range(0, rows, 8):
        turned = jnp.swapaxes(dens[r : r + 8], 0, 1)
        out[:, r : r + 8, :half] = turned[:levels]
        out[:, r : r + 8, half:] = turned[levels:]

    for side in range(2):
        row, inner, beyond, sign = places[side]

        @pl.when(has[side])
        def _():
            early_copy(side, side).wait_recv()
            late_copy(side, side).wait_recv()

        sum_x, sum_y, sum_xx, sum_xy, sum_yy = waiting[side]
        sum_y = sum_y - sign * early_in[side, 0]
        sum_xy = sum_xy - sign * early_in[side, 1]
        sum_yy = sum_yy + late_in[side]
        edge_row = density(sum_x, sum_y, sum_xx, sum_xy, sum_yy, count)
        for level in range(levels):
            out[level, row - 1 : row, :half] = edge_row[level : level + 1]
            out[level, row - 1 : row, half:] = edge_row[levels + level : levels + level + 1]

    for copy in slab_copies + halo_copies:
        copy.wait_send()
    for side in range(2):
        @pl.when(has[side])
        def _():
            for step in range(n):
                edge_copy(side, step).wait_send()
            early_copy(side, 1 - side).wait_send()
            late_copy(side, 1 - side).wait_send()


def per_device(n, tiles, winds):
    members, levels, parts, rows, lons = winds.shape
    width = lons // n
    half = width // 2
    pairs = members // 2
    size = 16 * rows
    assert levels == 4 and parts == 2 and members % 2 == 0 and rows % 8 == 0 and half % LANES == 0
    count = 9.0 * members * n
    groups = n * pairs
    dma = pltpu.SemaphoreType.DMA
    return pl.pallas_call(
        functools.partial(kernel, n, tiles, rows, pairs, count),
        out_shape=jax.ShapeDtypeStruct((levels, rows, width), jnp.float32),
        in_specs=[pl.BlockSpec(memory_space=pl.ANY)],
        out_specs=pl.BlockSpec(memory_space=pltpu.VMEM),
        scratch_shapes=[
            pltpu.VMEM((pairs * size, lons), jnp.bfloat16),
            pltpu.VMEM((max(n - 1, 1), pairs * size, width), jnp.bfloat16),
            pltpu.VMEM((n, pairs * size, LANES), jnp.bfloat16),
            pltpu.VMEM((max(n - 1, 1), pairs * size, LANES), jnp.bfloat16),
            pltpu.VMEM((2, 16, pairs * lons), jnp.bfloat16),
            pltpu.VMEM((2, n, 16, pairs * width + LANES), jnp.bfloat16),
            pltpu.VMEM((2, n, 16, pairs * width + LANES), jnp.bfloat16),
            pltpu.VMEM((groups, rows + 2, 8, width + LANES), jnp.float32),
            pltpu.VMEM((rows + 2, 8, half + LANES), jnp.float32),
            pltpu.VMEM((rows + 2, 8, half + LANES), jnp.float32),
            pltpu.VMEM((rows + 2, 8, half + LANES), jnp.float32),
            pltpu.VMEM((rows + 2, 8, half + LANES), jnp.float32),
            pltpu.VMEM((2, 2, 8, half), jnp.float32),
            pltpu.VMEM((2, 2, 8, half), jnp.float32),
            pltpu.VMEM((2, 8, half), jnp.float32),
            pltpu.VMEM((2, 8, half), jnp.float32),
            pltpu.VMEM((rows, 8, half), jnp.float32),
            dma((8,)), dma((n,)), dma((n,)), dma((n,)), dma((n,)),
            dma((2, n)), dma((2, n)), dma((2,)), dma((2,)), dma((2,)), dma((2,)),
        ],
        compiler_params=pltpu.CompilerParams(
            collective_id=0, has_side_effects=True, vmem_limit_bytes=60 * 2**20
        ),
    )(winds.reshape(pairs * size, lons))


def solution(mesh):
    return jax.shard_map(
        functools.partial(per_device, mesh.shape["member"], mesh.shape["tile"]),
        mesh=mesh,
        in_specs=(P("member", None, None, "tile", None),),
        out_specs=P(None, "tile", "member"),
        check_vma=False,
    )
```
